32 devices in a mesh: groups: 2 (over x), node: 8 (over z, y), local: 2 (over core).
Axes of the slice: x: 2, y: 2, z: 4, core: 2. Of those that a mesh axis runs over, the one named last changes fastest.
Arguments:
- tokens: bfloat16 [2, 1024, 3584], P(None, ('groups', 'node', 'local')), parts along dimension 1, may hold values from -6 to 6
- expert_ids: int32 [2, 1024, 4], P(None, ('groups', 'node', 'local')), parts along dimension 1, may hold values from 0 to 7, all different within a row; in each aligned block of 32 rows (0 to 31, 32 to 63, ..., all dimensions but the last counted through in order) at most 20 rows name the same one
- gate_fixed: int32 [2, 1024, 4], P(None, ('groups', 'node', 'local')), parts along dimension 1, may hold values from 6554 to 65536
- w_gate: bfloat16 [8, 3584, 1024], P('node', None, 'local'), may hold values from -0.09375 to 0.09375
- w_up: bfloat16 [8, 3584, 1024], P('node', None, 'local'), may hold values from -0.09375 to 0.09375
- w_down: bfloat16 [8, 1024, 3584], P('node', 'local'), may hold values from -0.1875 to 0.1875
Outputs:
- moe_out: bfloat16 [2, 1024, 3584], P(None, ('groups', 'node', 'local')), parts along dimension 1
The draws below stay inside these ranges and needn't reach their ends.
There are 2 independent parts, one for each index of `groups`. The reference program is written for one: setup_inputs(seed, part) draws one part's arguments, and reference() takes and returns one part's arrays. A program takes and returns all parts, laid end to end along the dimension named above; an argument that names none is the same for every part. Nothing has to cross between parts.
Inputs may be any that keep to these rules, and one draw needn't show every extreme that they name: `expert_ids`: each row names 4 different experts. Within each step, among the 32 rows of one device, no expert is named by more than 20 rows, a bound that some block reaches.
All inputs are finite; a program needn't handle non-finite values.
Results may differ from the reference program's by a relative error of at most 0.0057.
Values may be sent and summed in bfloat16 or wider, within the bound.
No kernel may reach another device: no remote copies, remote signals or barrier semaphores. Data moves between devices by JAX's collectives and lax.ppermute only.
A program may use at most 128 MiB of HBM per device.

```python
import math
import jax
import jax.numpy as jnp
import numpy as np
from jax import lax

D = 3584
FF = 1024
TOPK = 4
STEPS = 2
TOK_DEV = 32
EXPERTS = 8
CAP = 20
TOKENS = 512
N_NODE = 8
N_LOCAL = 2


def place_ends(result, rng, least, high):
    index_at = [jax.random.randint(jax.random.fold_in(rng, axis), (), 0, length) for axis, length in enumerate(result.shape)]
    main_axis = result.shape.index(max(result.shape))
    next_to = index_at[:main_axis] + [(index_at[main_axis] + 1) % result.shape[main_axis]] + index_at[main_axis + 1:]
    return result.at[tuple(index_at)].set(least).at[tuple(next_to)].set(high)


def steps_of(own_key, extent, shards, least, high):
    def one(dim, parts):
        steps = jax.random.uniform(jax.random.fold_in(jax.random.fold_in(own_key, 6), dim), (parts,), jnp.float32, least / len(shards), high / len(shards))
        return jnp.repeat(jnp.exp(steps), extent[dim] // parts).reshape((-1,) + (1,) * (len(extent) - dim - 1))

    level = one(*shards[0])
    for cut in shards[1:]:
        level = level * one(*cut)
    return level


def routed_block(key, own, number, rows, amount, top, most, slope):
    sequence = jax.random.permutation(key, amount)
    heavy_load, ordinary = shares(amount, rows * top, most, slope, True), shares(amount, rows * top, most, slope, False)
    places = jnp.arange(amount)

    def named(sizes, offset_by):
        used = int((sizes > 0).sum())
        fixed = max(1, used // 4)
        moved = fixed + (places - fixed + offset_by * (used - fixed)) % max(1, amount - fixed)
        return jnp.zeros((amount,), jnp.int32).at[sequence[jnp.where(places < fixed, places, moved)]].set(jnp.asarray(sizes, jnp.int32))

    sizes = jnp.where(number % 4 == 0, named(heavy_load, number // 4), named(ordinary, number - number // 4 - 1))
    mixed = jax.random.permutation(jax.random.fold_in(own, 3), amount)
    giver, receiver = mixed[0:amount // 2 * 2:2], mixed[1:amount // 2 * 2:2]
    margin = jnp.minimum(sizes[giver] - 1, most - sizes[receiver]) // 2
    margin = jnp.where((giver == sequence[0]) | (receiver == sequence[0]) | (sizes[receiver] == 0), 0, jnp.maximum(margin, 0))
    moved = jax.random.randint(jax.random.fold_in(own, 4), (amount // 2,), 0, 1 << 20) % (margin + 1)
    sizes = sizes.at[giver].add(-moved).at[receiver].add(moved)
    members = jnp.searchsorted(jnp.cumsum(sizes), jnp.arange(rows * top), side="right").astype(jnp.int32)
    grid = members.reshape(top, rows).T
    grid = grid[jax.random.permutation(jax.random.fold_in(own, 1), rows)]
    offset_by = jax.random.randint(jax.random.fold_in(own, 2), (rows, 1), 0, top)
    return jnp.take_along_axis(grid, (jnp.arange(top)[None, :] + offset_by) % top, axis=1)


def shares(count, total, bound, slope, full):
    weights = [(1 << 20) // math.isqrt(grade ** slope) + 1 for grade in range(1, count + 1)]
    largest = bound if full else min(bound, max(-(-total // count), total * weights[0] // sum(weights)))
    least = 1 if total - largest >= count - 1 else 0
    counts, rest = [largest] + [least] * (count - 1), total - largest - least * (count - 1)
    while rest > 0:
        movable = [i for i in range(1, count) if counts[i] < largest] or [i for i in range(1, count) if counts[i] < bound]
        mass, left = sum([weights[i] for i in movable]), rest
        for i in movable:
            more = min(bound - counts[i], max(1, left * weights[i] // mass), rest)
            counts[i] = counts[i] + more
            rest = rest - more
    return np.array(counts)


def noise(own_key, shape, scale, bound, cuts=(), held_as=jnp.bfloat16):
    drawn = scale * jax.random.normal(own_key, shape, jnp.float32)
    if cuts:
        drawn = drawn * steps_of(own_key, shape, cuts, -0.22, 0.18)
    return jnp.clip(drawn, -bound, bound).astype(held_as)


def setup_inputs(seed: int = 0, part: int = 0) -> dict:
    streams_of = jax.random.split(jax.random.key(seed), 7)
    part_keys = jax.random.split(jax.random.fold_in(streams_of[6], part), 7)
    tokens = noise(part_keys[0], (STEPS, TOKENS, D), 1.0, 6.0, ((1, 16),))
    expert_ids_keys = jax.random.split(jax.random.fold_in(part_keys[1], 1), STEPS * TOKENS // TOK_DEV)
    expert_ids_turns = jax.random.permutation(jax.random.fold_in(part_keys[1], 3), STEPS * TOKENS // TOK_DEV)
    expert_ids = jax.vmap(lambda own, number: routed_block(jax.random.fold_in(part_keys[1], 2), own, number, TOK_DEV, EXPERTS, TOPK, CAP, 2))(expert_ids_keys, expert_ids_turns).reshape((STEPS, TOKENS, TOPK))
    gate_fixed = place_ends(jax.random.randint(part_keys[2], (STEPS, TOKENS, TOPK), 6554, 65537), jax.random.fold_in(part_keys[2], 1), 6554, 65536).astype(jnp.int32)
    w_gate = noise(streams_of[3], (EXPERTS, D, FF), D ** -0.5, 0.09375, ((0, 8), (2, 2)))
    w_up = noise(streams_of[4], (EXPERTS, D, FF), D ** -0.5, 0.09375, ((0, 8), (2, 2)))
    w_down = noise(streams_of[5], (EXPERTS, FF, D), FF ** -0.5, 0.1875, ((0, 8), (1, 2)))
    return {"tokens": tokens, "expert_ids": expert_ids, "gate_fixed": gate_fixed, "w_gate": w_gate, "w_up": w_up, "w_down": w_down}


def expert_rows(picked, gate_mat, up_mat, down_mat):
    gate_act = jnp.dot(picked, gate_mat, preferred_element_type=jnp.float32)
    up_act = jnp.dot(picked, up_mat, preferred_element_type=jnp.float32)
    hidden = (jax.nn.silu(gate_act) * up_act).astype(jnp.bfloat16)
    return jnp.dot(hidden, down_mat, preferred_element_type=jnp.float32).astype(jnp.bfloat16)


def one_step(tokens_now, ids_now, fixed_now, w_gate, w_up, w_down):
    flat_ids = ids_now.reshape(-1).astype(jnp.int32)
    weights = fixed_now.reshape(-1).astype(jnp.float32) / 65536.0
    row_limit = N_NODE * N_LOCAL * CAP

    def add_expert(summed, expert):
        chosen = flat_ids == expert
        count = jnp.sum(chosen.astype(jnp.int32))
        picks = jnp.nonzero(chosen, size=row_limit, fill_value=0)[0].astype(jnp.int32)
        valid = jnp.arange(row_limit, dtype=jnp.int32) < count
        token_rows = picks // TOPK
        picked = jnp.take(tokens_now, token_rows, axis=0)
        outputs = expert_rows(picked, w_gate[expert], w_up[expert], w_down[expert])
        factor = jnp.where(valid, weights[picks], jnp.zeros_like(weights[picks]))
        summed = summed.at[token_rows].add(factor[:, None] * outputs.astype(jnp.float32))
        return summed, None

    start_sum = jnp.zeros(tokens_now.shape, jnp.float32)
    summed, _ = lax.scan(add_expert, start_sum, jnp.arange(EXPERTS, dtype=jnp.int32))
    return summed.astype(jnp.bfloat16)


def reference(tokens, expert_ids, gate_fixed, w_gate, w_up, w_down):
    results = [one_step(tokens[step_index], expert_ids[step_index], gate_fixed[step_index], w_gate, w_up, w_down) for step_index in range(STEPS)]
    return jnp.stack(results)
```

```python
import jax
import jax.numpy as jnp
from jax import lax
from jax.sharding import PartitionSpec as P


def ring_order(node_count, group_count):
    if group_count == 2:
        return list(range(0, node_count, 2)) + list(range(node_count - 1, 0, -2))
    return list(range(node_count))


def per_device(order, tokens, expert_ids, gate_fixed, w_gate, w_up, w_down):
    step_count, tok_rows, width = tokens.shape
    n = len(order)
    half = n // 2
    me = lax.axis_index("node")
    core = lax.axis_index("local")
    gate_mat, up_mat, down_mat = w_gate[0], w_up[0], w_down[0]

    def shift(value, distance):
        return lax.ppermute(value, "node", [(order[i], order[(i + distance) % n]) for i in range(n)])

    def swap(value):
        return lax.ppermute(value, "local", [(0, 1), (1, 0)])

    routes = jnp.stack([expert_ids, gate_fixed])
    routes = jnp.concatenate([routes.reshape(-1, 128), swap(routes.reshape(-1, 128))])
    route_from = {0: routes}
    for distance in range(1, n):
        route_from[distance] = shift(routes, distance)

    def weights_of(distance, step):
        table = route_from[distance % n].reshape(2, 2, step_count, tok_rows, -1)[:, :, step]
        hit = table[:, 0] == me
        return jnp.sum(jnp.where(hit, table[:, 1], 0), axis=-1).astype(jnp.float32) / 65536.0

    arrived = {(0, s): tokens[s] for s in range(step_count)}
    plus = {s: tokens[s] for s in range(step_count)}
    minus = dict(plus)
    for hop in range(1, half + 1):
        for s in range(step_count):
            if hop < half or s % 2 == 0:
                plus[s] = shift(plus[s], 1)
                arrived[hop, s] = plus[s]
            if hop < half or s % 2 == 1:
                minus[s] = shift(minus[s], -1)
                arrived[-hop if hop < half else hop, s] = minus[s]

    def experts(keys):
        rows = jnp.concatenate([arrived[k] for k in keys])
        other = swap(rows)
        factor = jnp.stack([weights_of(*k) for k in keys], axis=1).reshape(2, -1, 1)
        rows = jnp.concatenate([rows, other])
        factor = factor.reshape(-1, 1)
        gate_act = jnp.dot(rows, gate_mat, preferred_element_type=jnp.float32)
        up_act = jnp.dot(rows, up_mat, preferred_element_type=jnp.float32)
        hidden = (jax.nn.silu(gate_act) * up_act * factor).astype(jnp.bfloat16)
        part = jnp.dot(hidden, down_mat, preferred_element_type=jnp.float32)
        mine, theirs = jnp.split(part, 2)
        total = mine + swap(theirs.astype(jnp.bfloat16)).astype(jnp.float32)
        total = total.reshape(len(keys), tok_rows, width)
        return {k: total[i] for i, k in enumerate(keys)}

    partial = {}
    for hop in range(half + 1):
        places = [hop] if hop in (0, half) else [hop, -hop]
        partial.update(experts([(p, s) for p in places for s in range(step_count)]))

    def add(running, key):
        value = partial[key] if running is None else partial[key] + running.astype(jnp.float32)
        return value.astype(jnp.bfloat16)

    ahead = {s: None for s in range(step_count)}
    back = {s: None for s in range(step_count)}
    for hop in range(half, 0, -1):
        for s in range(step_count):
            if hop < half or s % 2 == 0:
                ahead[s] = shift(add(ahead[s], (-hop if hop < half else hop, s)), 1)
            if hop < half or s % 2 == 1:
                back[s] = shift(add(back[s], (hop, s)), -1)
    outputs = []
    for s in range(step_count):
        total = partial[0, s] + ahead[s].astype(jnp.float32) + back[s].astype(jnp.float32)
        outputs.append(total.astype(jnp.bfloat16))
    return jnp.stack(outputs)


def solution(mesh):
    order = ring_order(mesh.shape["node"], mesh.shape["groups"])
    rows = P(None, ("groups", "node", "local"), None)
    in_specs = (rows, rows, rows, P("node", None, "local"), P("node", None, "local"), P("node", "local", None))

    def call(*arrays):
        return per_device(order, *arrays)

    return jax.shard_map(call, mesh=mesh, in_specs=in_specs, out_specs=rows, check_vma=False)
```

```python
import functools

import jax
import jax.numpy as jnp
from jax import lax
from jax.experimental import pallas as pl
from jax.experimental.pallas import tpu as pltpu
from jax.sharding import PartitionSpec as P

TILE = 256
VMEM_LIMIT = 16 * 2**20
LANES = 128


def ring_order(node_count, group_count):
    if group_count == 2:
        return list(range(0, node_count, 2)) + list(range(node_count - 1, 0, -2))
    return list(range(node_count))


def experts_kernel(pieces, n, me, *refs):
    inputs, (w_gate, w_up, w_down) = refs[:pieces], refs[pieces : pieces + 3]
    mine, theirs, rows, hidden = refs[pieces + 3 :]
    width, units = w_gate.shape
    half = mine.shape[0]
    place = 0
    for piece in inputs:
        rows[pl.ds(place, piece.shape[0])] = piece[...]
        place += piece.shape[0]
    table = rows[:, width:].astype(jnp.float32)
    lane = lax.broadcasted_iota(jnp.int32, table.shape, 1)
    scale = jnp.where(lane == me[0], 1.0 / 256.0, jnp.where(lane == me[0] + n, 1.0 / 65536.0, 0.0))
    factor = jnp.sum(table * scale, axis=1, keepdims=True)
    for start in range(0, units, TILE):
        part = pl.ds(start, TILE)
        gate_act = jnp.dot(rows[:, :width], w_gate[:, part], preferred_element_type=jnp.float32)
        up_act = jnp.dot(rows[:, :width], w_up[:, part], preferred_element_type=jnp.float32)
        silu = gate_act / (1.0 + jnp.exp(-gate_act))
        hidden[:, part] = (silu * up_act * factor).astype(jnp.bfloat16)
    for start in range(0, width, TILE):
        part = pl.ds(start, TILE)
        product = jnp.dot(hidden[...], w_down[:, part], preferred_element_type=jnp.float32)
        mine[:, part] = product[:half].astype(mine.dtype)
        theirs[:, part] = product[half:].astype(jnp.bfloat16)


def run_experts(inputs, me, n, w_gate, w_up, w_down):
    total, message = sum(x.shape[0] for x in inputs), inputs[0].shape[1]
    width, units = w_gate.shape
    vmem = pl.BlockSpec(memory_space=pltpu.VMEM)
    return pl.pallas_call(
        functools.partial(experts_kernel, len(inputs), n),
        out_shape=(
            jax.ShapeDtypeStruct((total // 2, width), jnp.float32),
            jax.ShapeDtypeStruct((total // 2, width), jnp.bfloat16),
        ),
        in_specs=[pl.BlockSpec(memory_space=pltpu.SMEM)] + [vmem] * (len(inputs) + 3),
        out_specs=(vmem, vmem),
        scratch_shapes=[pltpu.VMEM((total, message), jnp.bfloat16), pltpu.VMEM((total, units), jnp.bfloat16)],
        compiler_params=pltpu.CompilerParams(vmem_limit_bytes=VMEM_LIMIT),
        cost_estimate=pl.CostEstimate(flops=6 * total * width * units, bytes_accessed=0, transcendentals=0),
    )(me, *inputs, w_gate, w_up, w_down)


def per_device(order, tokens, expert_ids, gate_fixed, w_gate, w_up, w_down):
    step_count, tok_rows, width = tokens.shape
    n = len(order)
    half = n // 2
    rows = step_count * tok_rows
    cut = step_count // 2 * tok_rows
    me = lax.axis_index("node").astype(jnp.int32).reshape(1)
    matrices = (w_gate[0], w_up[0], w_down[0])

    def shift(value, distance):
        return lax.ppermute(value, "node", [(order[i], order[(i + distance) % n]) for i in range(n)])

    def swap(value):
        return lax.ppermute(value, "local", [(0, 1), (1, 0)])

    experts = lax.broadcasted_iota(jnp.int32, (1, 1, n), 2)
    hit = expert_ids.reshape(rows, -1, 1) == experts
    weight = jnp.sum(jnp.where(hit, gate_fixed.reshape(rows, -1, 1), 0), axis=1)
    table = jnp.concatenate([weight >> 8, weight & 255], axis=1).astype(jnp.bfloat16)
    table = jnp.pad(table, ((0, 0), (0, -2 * n % LANES)))
    own = jnp.concatenate([tokens.reshape(rows, width), table], axis=1)

    plus, minus = shift(own, 1), shift(own, -1)
    results = {0: run_experts([own, swap(own)], me, n, *matrices)}
    for hop in range(1, half):
        plus, minus, results[hop - 1] = lax.optimization_barrier((plus, minus, results[hop - 1]))
        if hop + 1 < half:
            next_plus, next_minus = shift(plus, 1), shift(minus, -1)
        else:
            next_plus, next_minus = shift(plus[:cut], 1), shift(minus[cut:], -1)
        results[hop] = run_experts([plus, minus, swap(plus), swap(minus)], me, n, *matrices)
        plus, minus = next_plus, next_minus
    plus, minus, results[half - 1] = lax.optimization_barrier((plus, minus, results[half - 1]))
    results[half] = run_experts([plus, minus, swap(plus), swap(minus)], me, n, *matrices)

    def local_sum(hop):
        mine, theirs = results[hop]
        return mine + swap(theirs).astype(jnp.float32)

    far = local_sum(half).astype(jnp.bfloat16)
    ahead, back = shift(far[:cut], 1), shift(far[cut:], -1)
    for hop in range(half - 1, 0, -1):
        total = local_sum(hop)
        to_back, to_ahead = total[:rows], total[rows:]
        if hop == half - 1:
            ahead = jnp.concatenate([to_ahead[:cut] + ahead.astype(jnp.float32), to_ahead[cut:]])
            back = jnp.concatenate([to_back[:cut], to_back[cut:] + back.astype(jnp.float32)])
        else:
            ahead = to_ahead + ahead.astype(jnp.float32)
            back = to_back + back.astype(jnp.float32)
        ahead, back = shift(ahead.astype(jnp.bfloat16), 1), shift(back.astype(jnp.bfloat16), -1)
    total = local_sum(0) + ahead.astype(jnp.float32) + back.astype(jnp.float32)
    return total.astype(jnp.bfloat16).reshape(tokens.shape)


def solution(mesh):
    order = ring_order(mesh.shape["node"], mesh.shape["groups"])
    rows = P(None, ("groups", "node", "local"), None)
    in_specs = (rows, rows, rows, P("node", None, "local"), P("node", None, "local"), P("node", "local", None))
    return jax.shard_map(
        functools.partial(per_device, order), mesh=mesh, in_specs=in_specs, out_specs=rows, check_vma=False
    )
```

```python
import functools

import jax
import jax.numpy as jnp
from jax import lax
from jax.experimental import pallas as pl
from jax.experimental.pallas import tpu as pltpu
from jax.sharding import PartitionSpec as P

TILE = 256
LANES = 128
LEAST_ROWS = 128
VMEM_LIMIT = 12 * 2**20
VMEM = pl.BlockSpec(memory_space=pltpu.VMEM)
PARAMS = pltpu.CompilerParams(vmem_limit_bytes=VMEM_LIMIT)
NO_COST = pl.CostEstimate(flops=0, bytes_accessed=0, transcendentals=0)


def ring_order(node_count, group_count):
    if group_count == 2:
        return list(range(0, node_count, 2)) + list(range(node_count - 1, 0, -2))
    return list(range(node_count))


def message_kernel(n, tokens, routes, message, semaphore):
    rows, width = tokens.shape
    copy = pltpu.make_async_copy(tokens, message.at[:, pl.ds(0, width)], semaphore)
    copy.start()
    lane = lax.broadcasted_iota(jnp.int32, (rows, message.shape[1] - width), 1)
    table = jnp.zeros(lane.shape, jnp.int32)
    for k in range(routes.shape[3]):
        expert, weight = (routes[i, :, :, k : k + 1].reshape(rows, 1) for i in range(2))
        table += jnp.where(lane == expert, weight >> 8, 0) + jnp.where(lane == expert + n, weight & 255, 0)
    message[:, width:] = table.astype(jnp.float32).astype(jnp.bfloat16)
    copy.wait()


def make_message(n, tokens, expert_ids, gate_fixed):
    rows, width = tokens.shape
    routes = jnp.stack([expert_ids, gate_fixed])
    return pl.pallas_call(
        functools.partial(message_kernel, n),
        out_shape=jax.ShapeDtypeStruct((rows, width + -(-2 * n // LANES) * LANES), jnp.bfloat16),
        in_specs=[pl.BlockSpec(memory_space=pl.ANY), VMEM],
        out_specs=VMEM,
        scratch_shapes=[pltpu.SemaphoreType.DMA],
        compiler_params=PARAMS,
        cost_estimate=NO_COST,
    )(tokens, routes)


def experts_kernel(pieces, n, me, *refs):
    inputs, matrices, outputs, (rows, hidden) = refs[:pieces], refs[pieces : pieces + 6], refs[pieces + 6 : -2], refs[-2:]
    width, units = matrices[0].shape
    place = 0
    for piece in inputs:
        rows[pl.ds(place, piece.shape[0])] = piece[...]
        place += piece.shape[0]
    table = rows[:, width:].astype(jnp.float32)
    lane = lax.broadcasted_iota(jnp.int32, table.shape, 1)
    scale = jnp.where(lane == me[0], 1.0 / 256.0, jnp.where(lane == me[0] + n, 1.0 / 65536.0, 0.0))
    factor = jnp.sum(table * scale, axis=1, keepdims=True)
    for side in range(2):
        w_gate, w_up = matrices[3 * side : 3 * side + 2]
        for start in range(0, units, TILE):
            part = pl.ds(start, TILE)
            gate_act = jnp.dot(rows[:, :width], w_gate[:, part], preferred_element_type=jnp.float32)
            up_act = jnp.dot(rows[:, :width], w_up[:, part], preferred_element_type=jnp.float32)
            silu = gate_act / (1.0 + jnp.exp(-gate_act))
            hidden[:, pl.ds(side * units + start, TILE)] = (silu * up_act * factor).astype(jnp.bfloat16)
    for start in range(0, width, TILE):
        part = pl.ds(start, TILE)
        product = jnp.dot(hidden[:, :units], matrices[2][:, part], preferred_element_type=jnp.float32)
        product += jnp.dot(hidden[:, units:], matrices[5][:, part], preferred_element_type=jnp.float32)
        place = 0
        for output in outputs:
            output[:, part] = product[place : place + output.shape[0]].astype(output.dtype)
            place += output.shape[0]


def run_experts(inputs, kinds, me, n, matrices):
    total, message = sum(x.shape[0] for x in inputs), inputs[0].shape[1]
    width, units = matrices[0].shape
    held = max(total, LEAST_ROWS)
    return pl.pallas_call(
        functools.partial(experts_kernel, len(inputs), n),
        out_shape=[jax.ShapeDtypeStruct((total // len(kinds), width), kind) for kind in kinds],
        in_specs=[pl.BlockSpec(memory_space=pltpu.SMEM)] + [VMEM] * (len(inputs) + 6),
        out_specs=[VMEM] * len(kinds),
        scratch_shapes=[pltpu.VMEM((held, message), jnp.bfloat16), pltpu.VMEM((held, 2 * units), jnp.bfloat16)],
        compiler_params=PARAMS,
        cost_estimate=NO_COST,
    )(me, *inputs, *matrices)


def keep_kernel(source, to, semaphore):
    copy = pltpu.make_async_copy(source, to, semaphore)
    copy.start()
    copy.wait()


def keep(value):
    return pl.pallas_call(
        keep_kernel,
        out_shape=jax.ShapeDtypeStruct(value.shape, value.dtype),
        in_specs=[pl.BlockSpec(memory_space=pl.ANY)],
        out_specs=VMEM,
        scratch_shapes=[pltpu.SemaphoreType.DMA],
        compiler_params=PARAMS,
        cost_estimate=NO_COST,
    )(value)


def add_kernel(*refs):
    refs[-1][...] = sum(ref[...].astype(jnp.float32) for ref in refs[:-1]).astype(jnp.bfloat16)


def add_up(*terms):
    return pl.pallas_call(
        add_kernel,
        out_shape=jax.ShapeDtypeStruct(terms[0].shape, jnp.bfloat16),
        in_specs=[VMEM] * len(terms),
        out_specs=VMEM,
        compiler_params=PARAMS,
        cost_estimate=NO_COST,
    )(*terms)


def finish_kernel(count, *refs):
    terms, out, sums, semaphores = refs[:-3], refs[-3], refs[-2], refs[-1]
    copies = []
    for s in range(count):
        sums[s] = sum(ref[...].astype(jnp.float32) for ref in terms[3 * s : 3 * s + 3]).astype(jnp.bfloat16)
        copies.append(pltpu.make_async_copy(sums.at[s], out.at[s], semaphores.at[s]))
        copies[-1].start()
    for copy in copies:
        copy.wait()


def finish(terms):
    shape = (len(terms), *terms[0][0].shape)
    return pl.pallas_call(
        functools.partial(finish_kernel, len(terms)),
        out_shape=jax.ShapeDtypeStruct(shape, jnp.bfloat16),
        in_specs=[VMEM] * (3 * len(terms)),
        out_specs=pl.BlockSpec(memory_space=pl.ANY),
        scratch_shapes=[pltpu.VMEM(shape, jnp.bfloat16), pltpu.SemaphoreType.DMA((len(terms),))],
        compiler_params=PARAMS,
        cost_estimate=NO_COST,
    )(*sum(terms, ()))


def per_device(order, tokens, expert_ids, gate_fixed, w_gate, w_up, w_down):
    step_count, tok_rows, width = tokens.shape
    steps = range(step_count)
    n = len(order)
    half = n // 2
    me = lax.axis_index("node").astype(jnp.int32).reshape(1)

    def shift(value, distance):
        return lax.ppermute(value, "node", [(order[i], order[(i + distance) % n]) for i in range(n)])

    def swap(value):
        return lax.ppermute(value, "local", [(0, 1), (1, 0)])

    def in_order(*arrays):
        nonlocal me
        me, *arrays = lax.optimization_barrier((me, *arrays))
        return arrays

    def far_ahead(s):
        return s % 2 == 0

    own = make_message(n, tokens.reshape(step_count * tok_rows, width), expert_ids, gate_fixed)
    whole = [shift(own, 1), shift(own, -1)]
    matrices = [w_gate[0], w_up[0], w_down[0]]
    arriving = [swap(matrix) for matrix in matrices]
    outputs = {}

    def load(count):
        for _ in range(count):
            matrices.extend(in_order(keep(*in_order(arriving.pop(0)))))

    def work(names, rows, kinds={}):
        kinds = [kinds.get(name, jnp.float32) for name in names]
        outputs.update(zip(names, in_order(*run_experts(in_order(*rows), kinds, me, n, matrices))))

    load(2)
    whole = in_order(*whole)
    came = {0: ([("own", 0, s) for s in steps], [own]), 1: ([(side, 1, s) for side in ("back", "ahead") for s in steps], whole)}
    plus, minus = {}, {}
    for s in steps:
        part = slice(s * tok_rows, (s + 1) * tok_rows)
        plus[s], minus[s] = shift(whole[0][part], 1), shift(whole[1][part], -1)
    load(1)
    for hop in range(2, half):
        came[hop] = ([], [])
        for s in steps:
            if s == step_count - 1 and hop > 2:
                work(*came.pop(hop - 1))
            plus[s], minus[s] = in_order(plus[s], minus[s])
            came[hop] = (came[hop][0] + [("back", hop, s), ("ahead", hop, s)], came[hop][1] + [plus[s], minus[s]])
            if hop + 1 < half or far_ahead(s):
                plus[s] = shift(plus[s], 1)
            if hop + 1 < half or not far_ahead(s):
                minus[s] = shift(minus[s], -1)
        if hop == 2:
            work(*came.pop(1))
    came[half] = ([("far", half, s) for s in steps], [plus[s] if far_ahead(s) else minus[s] for s in steps])

    longer = {s: ("ahead", 1) if far_ahead(s) else ("back", -1) for s in steps}
    shorter = {s: ("back", -1) if far_ahead(s) else ("ahead", 1) for s in steps}
    long, short = {}, {}
    work(*came[half - 1], {(shorter[s][0], half - 1, s): jnp.bfloat16 for s in steps})
    for s in steps:
        short[s] = shift(outputs[shorter[s][0], half - 1, s], shorter[s][1])
    work(*came[half], {("far", half, s): jnp.bfloat16 for s in steps})
    for s in steps:
        long[s] = shift(outputs["far", half, s], longer[s][1])

    def pass_on(sums, ways, hop):
        for s in steps:
            side, way = ways[s]
            sums[s] = shift(add_up(outputs[side, hop, s], sums[s]), way)

    for hop in range(half - 2, -1, -1):
        if hop == 0:
            outputs.update(zip(came[0][0], run_experts(came[0][1], [jnp.float32] * step_count, me, n, matrices)))
        else:
            pass_on(short, shorter, hop)
        pass_on(long, longer, hop + 1)
    return finish([(outputs["own", 0, s], short[s], long[s]) for s in steps])


def solution(mesh):
    order = ring_order(mesh.shape["node"], mesh.shape["groups"])
    rows = P(None, ("groups", "node", "local"), None)
    in_specs = (rows, rows, rows, P("node", None, "local"), P("node", None, "local"), P("node", "local", None))
    return jax.shard_map(
        functools.partial(per_device, order), mesh=mesh, in_specs=in_specs, out_specs=rows, check_vma=False
    )
```

```python
import functools

import jax
import jax.numpy as jnp
from jax import lax
from jax.experimental import pallas as pl
from jax.experimental.pallas import tpu as pltpu
from jax.sharding import PartitionSpec as P

TILE = 256
LANES = 128
LEAST_ROWS = 128
VMEM_LIMIT = 12 * 2**20
VMEM = pl.BlockSpec(memory_space=pltpu.VMEM)
PARAMS = pltpu.CompilerParams(vmem_limit_bytes=VMEM_LIMIT)
NO_COST = pl.CostEstimate(flops=0, bytes_accessed=0, transcendentals=0)


def ring_order(node_count, group_count):
    if group_count == 2:
        return list(range(0, node_count, 2)) + list(range(node_count - 1, 0, -2))
    return list(range(node_count))


def message_kernel(n, tokens, routes, message, semaphore):
    rows, width = tokens.shape
    copy = pltpu.make_async_copy(tokens, message.at[:, pl.ds(0, width)], semaphore)
    copy.start()
    lane = lax.broadcasted_iota(jnp.int32, (rows, message.shape[1] - width), 1)
    table = jnp.zeros(lane.shape, jnp.int32)
    for k in range(routes.shape[3]):
        expert, weight = (routes[i, :, :, k : k + 1].reshape(rows, 1) for i in range(2))
        table += jnp.where(lane == expert, weight >> 8, 0) + jnp.where(lane == expert + n, weight & 255, 0)
    message[:, width:] = table.astype(jnp.float32).astype(jnp.bfloat16)
    copy.wait()


def make_message(n, tokens, expert_ids, gate_fixed):
    rows, width = tokens.shape
    routes = jnp.stack([expert_ids, gate_fixed])
    return pl.pallas_call(
        functools.partial(message_kernel, n),
        out_shape=jax.ShapeDtypeStruct((rows, width + -(-2 * n // LANES) * LANES), jnp.bfloat16),
        in_specs=[pl.BlockSpec(memory_space=pl.ANY), VMEM],
        out_specs=VMEM,
        scratch_shapes=[pltpu.SemaphoreType.DMA],
        compiler_params=PARAMS,
        cost_estimate=NO_COST,
    )(tokens, routes)


def experts_kernel(pieces, n, me, *refs):
    inputs, matrices, outputs, (rows, hidden) = refs[:pieces], refs[pieces : pieces + 6], refs[pieces + 6 : -2], refs[-2:]
    width, units = matrices[0].shape
    place = 0
    for piece in inputs:
        rows[pl.ds(place, piece.shape[0])] = piece[...]
        place += piece.shape[0]
    table = rows[:, width:].astype(jnp.float32)
    lane = lax.broadcasted_iota(jnp.int32, table.shape, 1)
    scale = jnp.where(lane == me[0], 1.0 / 256.0, jnp.where(lane == me[0] + n, 1.0 / 65536.0, 0.0))
    factor = jnp.sum(table * scale, axis=1, keepdims=True)
    for side in range(2):
        w_gate, w_up = matrices[3 * side : 3 * side + 2]
        for start in range(0, units, TILE):
            part = pl.ds(start, TILE)
            gate_act = jnp.dot(rows[:, :width], w_gate[:, part], preferred_element_type=jnp.float32)
            up_act = jnp.dot(rows[:, :width], w_up[:, part], preferred_element_type=jnp.float32)
            silu = gate_act / (1.0 + jnp.exp(-gate_act))
            hidden[:, pl.ds(side * units + start, TILE)] = (silu * up_act * factor).astype(jnp.bfloat16)
    for start in range(0, width, TILE):
        part = pl.ds(start, TILE)
        product = jnp.dot(hidden[:, :units], matrices[2][:, part], preferred_element_type=jnp.float32)
        product += jnp.dot(hidden[:, units:], matrices[5][:, part], preferred_element_type=jnp.float32)
        place = 0
        for output in outputs:
            output[:, part] = product[place : place + output.shape[0]].astype(output.dtype)
            place += output.shape[0]


def run_experts(inputs, kinds, me, n, matrices):
    total, message = sum(x.shape[0] for x in inputs), inputs[0].shape[1]
    width, units = matrices[0].shape
    held = max(total, LEAST_ROWS)
    return pl.pallas_call(
        functools.partial(experts_kernel, len(inputs), n),
        out_shape=[jax.ShapeDtypeStruct((total // len(kinds), width), kind) for kind in kinds],
        in_specs=[pl.BlockSpec(memory_space=pltpu.SMEM)] + [VMEM] * (len(inputs) + 6),
        out_specs=[VMEM] * len(kinds),
        scratch_shapes=[pltpu.VMEM((held, message), jnp.bfloat16), pltpu.VMEM((held, 2 * units), jnp.bfloat16)],
        compiler_params=PARAMS,
        cost_estimate=NO_COST,
    )(me, *inputs, *matrices)


def keep_kernel(source, to, semaphore):
    copy = pltpu.make_async_copy(source, to, semaphore)
    copy.start()
    copy.wait()


def keep(value):
    return pl.pallas_call(
        keep_kernel,
        out_shape=jax.ShapeDtypeStruct(value.shape, value.dtype),
        in_specs=[pl.BlockSpec(memory_space=pl.ANY)],
        out_specs=VMEM,
        scratch_shapes=[pltpu.SemaphoreType.DMA],
        compiler_params=PARAMS,
        cost_estimate=NO_COST,
    )(value)


def add_kernel(places, mine, came, *sums):
    size = sums[0].shape[0]
    for place, to in zip(places, sums):
        here = pl.ds(place * size, size)
        there = here if came.shape == mine.shape else slice(None)
        to[...] = (mine[here] + came[there].astype(jnp.float32)).astype(jnp.bfloat16)


def add_up(terms, parts=1, only=None):
    mine, came = terms
    places = range(parts) if only is None else [only]
    part = jax.ShapeDtypeStruct((mine.shape[0] // parts, mine.shape[1]), jnp.bfloat16)
    return pl.pallas_call(
        functools.partial(add_kernel, places),
        out_shape=[part] * len(places),
        in_specs=[VMEM] * 2,
        out_specs=[VMEM] * len(places),
        compiler_params=PARAMS,
        cost_estimate=NO_COST,
    )(mine, came)


def finish_kernel(mine, other, *refs):
    parts, out, total, semaphores = refs[:-3], refs[-3], refs[-2], refs[-1]
    size = parts[0].shape[0]
    copies = []
    for i, part in enumerate(parts):
        here = pl.ds(i * size, size)
        total[here] = (mine[here] + other[here].astype(jnp.float32) + part[...].astype(jnp.float32)).astype(jnp.bfloat16)
        copies.append(pltpu.make_async_copy(total.at[here], out.at[here], semaphores.at[i]))
        copies[-1].start()
    for copy in copies:
        copy.wait()


def finish(mine, other, *parts):
    return pl.pallas_call(
        finish_kernel,
        out_shape=jax.ShapeDtypeStruct(mine.shape, jnp.bfloat16),
        in_specs=[VMEM] * (2 + len(parts)),
        out_specs=pl.BlockSpec(memory_space=pl.ANY),
        scratch_shapes=[pltpu.VMEM(mine.shape, jnp.bfloat16), pltpu.SemaphoreType.DMA((len(parts),))],
        compiler_params=PARAMS,
        cost_estimate=NO_COST,
    )(mine, other, *parts)


def per_device(order, tokens, expert_ids, gate_fixed, w_gate, w_up, w_down):
    step_count, tok_rows, width = tokens.shape
    n = len(order)
    half = n // 2
    me = lax.axis_index("node").astype(jnp.int32).reshape(1)
    ring = [(2 * order[i] + core, 2 * order[(i + 1 - 2 * core) % n] + core) for i in range(n) for core in range(2)]

    def onward(value):
        return lax.ppermute(value, ("node", "local"), ring)

    def home(value):
        return lax.ppermute(value, ("node", "local"), [(to, source) for source, to in ring])

    def swap(value):
        return lax.ppermute(value, "local", [(0, 1), (1, 0)])

    def in_order(*arrays):
        nonlocal me
        me, *arrays = lax.optimization_barrier((me, *arrays))
        return arrays

    own = make_message(n, tokens.reshape(step_count * tok_rows, width), expert_ids, gate_fixed)
    other = swap(own)
    long, short = onward(own), onward(other)
    matrices = [w_gate[0], w_up[0], w_down[0]]
    arriving = [swap(lax.optimization_barrier((other, matrix))[1]) for matrix in matrices]
    outputs = {}

    def load():
        matrices.extend(in_order(keep(*in_order(arriving.pop(0)))))

    def work(hop, kinds, ordered=True):
        rows = came[hop]
        results = run_experts(in_order(*rows) if ordered else rows, kinds, me, n, matrices)
        outputs[hop] = in_order(*results) if ordered else results

    came = {0: [own]}
    for hop in range(1, half):
        (first,) = in_order(long)
        long = onward(first)
        if hop <= 2:
            load()
        else:
            work(hop - 1, [jnp.float32] * 2)
        (second,) = in_order(short)
        if hop + 1 < half:
            short = onward(second)
        came[hop] = [first, second]
        if hop == 1:
            load()
        elif hop == 2:
            work(1, [jnp.float32] * 2)
    came[half] = [long]

    work(half - 1, [jnp.float32, jnp.bfloat16])
    short = home(outputs[half - 1][1])
    work(half, [jnp.bfloat16])
    long = home(outputs[half][0])
    for hop in range(half - 1, 0, -1):
        if hop > 1:
            short = home(add_up([outputs[hop - 1][1], short])[0])
        if hop > 2:
            long = home(add_up([outputs[hop][0], long])[0])
        elif hop == 2:
            long = [home(part) for part in add_up([outputs[hop][0], long], 2)]
        else:
            long = [home(add_up([outputs[hop][0], part], 2, i)[0]) for i, part in enumerate(long)]
    work(0, [jnp.float32], False)
    return finish(outputs[0][0], swap(short), *long).reshape(tokens.shape)


def solution(mesh):
    order = ring_order(mesh.shape["node"], mesh.shape["groups"])
    rows = P(None, ("groups", "node", "local"), None)
    in_specs = (rows, rows, rows, P("node", None, "local"), P("node", None, "local"), P("node", "local", None))
    return jax.shard_map(
        functools.partial(per_device, order), mesh=mesh, in_specs=in_specs, out_specs=rows, check_vma=False
    )
```

```python
import functools

import jax
import jax.numpy as jnp
from jax import lax
from jax.experimental import pallas as pl
from jax.experimental.pallas import tpu as pltpu
from jax.sharding import PartitionSpec as P

TILE = 512
LANES = 128
LEAST_ROWS = 128
VMEM_LIMIT = 12 * 2**20
VMEM = pl.BlockSpec(memory_space=pltpu.VMEM)
PARAMS = pltpu.CompilerParams(vmem_limit_bytes=VMEM_LIMIT)
NO_COST = pl.CostEstimate(flops=0, bytes_accessed=0, transcendentals=0)


def ring_order(node_count, group_count):
    if group_count == 2:
        return list(range(0, node_count, 2)) + list(range(node_count - 1, 0, -2))
    return list(range(node_count))


def message_kernel(n, tokens, routes, message, semaphore):
    rows, width = tokens.shape
    copy = pltpu.make_async_copy(tokens, message.at[:, pl.ds(0, width)], semaphore)
    copy.start()
    lane = lax.broadcasted_iota(jnp.int32, (rows, message.shape[1] - width), 1)
    table = jnp.zeros(lane.shape, jnp.int32)
    steps = routes.shape[0] // 2
    for k in range(routes.shape[2]):
        expert, weight = (routes[i * steps : (i + 1) * steps, :, k : k + 1].reshape(rows, 1) for i in range(2))
        table += jnp.where(lane == expert, weight >> 8, 0) + jnp.where(lane == expert + n, weight & 255, 0)
    message[:, width:] = table.astype(jnp.float32).astype(jnp.bfloat16)
    copy.wait()


def make_message(n, tokens, expert_ids, gate_fixed):
    rows, width = tokens.shape
    routes = jnp.concatenate([expert_ids, gate_fixed])
    return pl.pallas_call(
        functools.partial(message_kernel, n),
        out_shape=jax.ShapeDtypeStruct((rows, width + -(-2 * n // LANES) * LANES), jnp.bfloat16),
        in_specs=[pl.BlockSpec(memory_space=pl.ANY), VMEM],
        out_specs=VMEM,
        scratch_shapes=[pltpu.SemaphoreType.DMA],
        compiler_params=PARAMS,
        cost_estimate=NO_COST,
    )(tokens, routes)


def experts_kernel(pieces, n, me, *refs):
    inputs, matrices, outputs, (rows, hidden) = refs[:pieces], refs[pieces : pieces + 6], refs[pieces + 6 : -2], refs[-2:]
    width, units = matrices[0].shape
    place = 0
    for piece in inputs:
        rows[pl.ds(place, piece.shape[0])] = piece[...]
        place += piece.shape[0]
    table = rows[:, width:].astype(jnp.float32)
    lane = lax.broadcasted_iota(jnp.int32, table.shape, 1)
    scale = jnp.where(lane == me[0], 1.0 / 256.0, jnp.where(lane == me[0] + n, 1.0 / 65536.0, 0.0))
    factor = jnp.sum(table * scale, axis=1, keepdims=True)
    for side in range(2):
        w_gate, w_up = matrices[3 * side : 3 * side + 2]
        for start in range(0, units, TILE):
            part = pl.ds(start, TILE)
            gate_act = jnp.dot(rows[:, :width], w_gate[:, part], preferred_element_type=jnp.float32)
            up_act = jnp.dot(rows[:, :width], w_up[:, part], preferred_element_type=jnp.float32)
            silu = gate_act / (1.0 + jnp.exp(-gate_act))
            hidden[:, pl.ds(side * units + start, TILE)] = (silu * up_act * factor).astype(jnp.bfloat16)
    for start in range(0, width, TILE):
        part = pl.ds(start, TILE)
        product = jnp.dot(hidden[:, :units], matrices[2][:, part], preferred_element_type=jnp.float32)
        product += jnp.dot(hidden[:, units:], matrices[5][:, part], preferred_element_type=jnp.float32)
        place = 0
        for output in outputs:
            output[:, part] = product[place : place + output.shape[0]].astype(output.dtype)
            place += output.shape[0]


def run_experts(inputs, kinds, me, n, matrices):
    total, message = sum(x.shape[0] for x in inputs), inputs[0].shape[1]
    width, units = matrices[0].shape
    held = max(total, LEAST_ROWS)
    return pl.pallas_call(
        functools.partial(experts_kernel, len(inputs), n),
        out_shape=[jax.ShapeDtypeStruct((total // len(kinds), width), kind) for kind in kinds],
        in_specs=[pl.BlockSpec(memory_space=pltpu.SMEM)] + [VMEM] * (len(inputs) + 6),
        out_specs=[VMEM] * len(kinds),
        scratch_shapes=[pltpu.VMEM((held, message), jnp.bfloat16), pltpu.VMEM((held, 2 * units), jnp.bfloat16)],
        compiler_params=PARAMS,
        cost_estimate=NO_COST,
    )(me, *inputs, *matrices)


def keep_kernel(source, to, semaphore):
    copy = pltpu.make_async_copy(source, to, semaphore)
    copy.start()
    copy.wait()


def keep(value):
    return pl.pallas_call(
        keep_kernel,
        out_shape=jax.ShapeDtypeStruct(value.shape, value.dtype),
        in_specs=[pl.BlockSpec(memory_space=pl.ANY)],
        out_specs=VMEM,
        scratch_shapes=[pltpu.SemaphoreType.DMA],
        compiler_params=PARAMS,
        cost_estimate=NO_COST,
    )(value)


def add_kernel(places, mine, came, *sums):
    size = sums[0].shape[0]
    for place, to in zip(places, sums):
        here = pl.ds(place * size, size)
        there = here if came.shape == mine.shape else slice(None)
        to[...] = (mine[here] + came[there].astype(jnp.float32)).astype(jnp.bfloat16)


def add_up(terms, parts=1, only=None):
    mine, came = terms
    places = range(parts) if only is None else [only]
    part = jax.ShapeDtypeStruct((mine.shape[0] // parts, mine.shape[1]), jnp.bfloat16)
    return pl.pallas_call(
        functools.partial(add_kernel, places),
        out_shape=[part] * len(places),
        in_specs=[VMEM] * 2,
        out_specs=[VMEM] * len(places),
        compiler_params=PARAMS,
        cost_estimate=NO_COST,
    )(mine, came)


def finish_kernel(mine, other, *refs):
    parts, out, total, semaphores = refs[:-3], refs[-3], refs[-2], refs[-1]
    size = parts[0].shape[0]
    copies = []
    for i, part in enumerate(parts):
        here = pl.ds(i * size, size)
        total[here] = (mine[here] + other[here].astype(jnp.float32) + part[...].astype(jnp.float32)).astype(jnp.bfloat16)
        copies.append(pltpu.make_async_copy(total.at[here], out.at[here], semaphores.at[i]))
        copies[-1].start()
    for copy in copies:
        copy.wait()


def finish(mine, other, *parts):
    return pl.pallas_call(
        finish_kernel,
        out_shape=jax.ShapeDtypeStruct(mine.shape, jnp.bfloat16),
        in_specs=[VMEM] * (2 + len(parts)),
        out_specs=pl.BlockSpec(memory_space=pl.ANY),
        scratch_shapes=[pltpu.VMEM(mine.shape, jnp.bfloat16), pltpu.SemaphoreType.DMA((len(parts),))],
        compiler_params=PARAMS,
        cost_estimate=NO_COST,
    )(mine, other, *parts)


def per_device(order, tokens, expert_ids, gate_fixed, w_gate, w_up, w_down):
    step_count, tok_rows, width = tokens.shape
    n = len(order)
    half = n // 2
    me = lax.axis_index("node").astype(jnp.int32).reshape(1)
    ring = [(2 * order[i] + core, 2 * order[(i + 1 - 2 * core) % n] + core) for i in range(n) for core in range(2)]

    def onward(value):
        return lax.ppermute(value, ("node", "local"), ring)

    def home(value):
        return lax.ppermute(value, ("node", "local"), [(to, source) for source, to in ring])

    def swap(value):
        return lax.ppermute(value, "local", [(0, 1), (1, 0)])

    def in_order(*arrays):
        nonlocal me
        me, *arrays = lax.optimization_barrier((me, *arrays))
        return arrays

    own = make_message(n, tokens.reshape(step_count * tok_rows, width), expert_ids, gate_fixed)
    other = swap(own)
    long, short = onward(own), onward(other)
    matrices = [w_gate[0], w_up[0], w_down[0]]
    arriving = [swap(lax.optimization_barrier((other, matrix))[1]) for matrix in matrices]
    outputs = {}

    def load():
        matrices.extend(in_order(keep(*in_order(arriving.pop(0)))))

    def work(hop, kinds, ordered=True):
        rows = came[hop]
        results = run_experts(in_order(*rows) if ordered else rows, kinds, me, n, matrices)
        outputs[hop] = in_order(*results) if ordered else results

    came = {0: [own]}
    for hop in range(1, half):
        (first,) = in_order(long)
        long = onward(first)
        if hop <= 2:
            load()
        else:
            work(hop - 1, [jnp.float32] * 2)
        (second,) = in_order(short)
        if hop + 1 < half:
            short = onward(second)
        came[hop] = [first, second]
        if hop == 1:
            load()
        elif hop == 2:
            work(1, [jnp.float32] * 2)
    came[half] = [long]

    work(half - 1, [jnp.float32, jnp.bfloat16])
    short = home(outputs[half - 1][1])
    work(half, [jnp.bfloat16])
    long = home(outputs[half][0])
    for hop in range(half - 1, 0, -1):
        if hop > 1:
            short = home(add_up([outputs[hop - 1][1], short])[0])
        if hop > 2:
            long = home(add_up([outputs[hop][0], long])[0])
        elif hop == 2:
            long = [home(part) for part in add_up([outputs[hop][0], long], 2)]
        else:
            long = [home(add_up([outputs[hop][0], part], 2, i)[0]) for i, part in enumerate(long)]
    work(0, [jnp.float32], False)
    return finish(outputs[0][0], swap(short), *long).reshape(tokens.shape)


def solution(mesh):
    order = ring_order(mesh.shape["node"], mesh.shape["groups"])
    rows = P(None, ("groups", "node", "local"), None)
    in_specs = (rows, rows, rows, P("node", None, "local"), P("node", None, "local"), P("node", "local", None))
    return jax.shard_map(
        functools.partial(per_device, order), mesh=mesh, in_specs=in_specs, out_specs=rows, check_vma=False
    )
```
